512 devices in a mesh: dp: 32 (over x, z), ctx: 16 (over y, core).
Axes of the slice: x: 4, y: 8, z: 8, core: 2. Of those that a mesh axis runs over, the one named last changes fastest.
Arguments:
- query: bfloat16 [65536, 2048], P(('dp', 'ctx')), parts along dimension 0, may hold values from -24 to 24
- key: bfloat16 [65536, 512], P(('dp', 'ctx')), parts along dimension 0, may hold values from -7.5 to 7.5
- value: bfloat16 [65536, 512], P(('dp', 'ctx')), parts along dimension 0, may hold values from -6 to 6
- output_gradient: bfloat16 [65536, 2048], P(('dp', 'ctx')), parts along dimension 0, may hold values from -6 to 6
- doc_blocks: int32 [512], P('dp'), parts along dimension 0, may hold values from 0 to 2, never falling along the last dimension, each value on 1 to 11 neighbouring positions
- shard_order: int32 [512], P('dp'), parts along dimension 0, may hold values from 0 to 15, as said below
Outputs:
- attn_out: bfloat16 [65536, 2048], P(('dp', 'ctx')), parts along dimension 0
- grad_query: bfloat16 [65536, 2048], P(('dp', 'ctx')), parts along dimension 0
- key_gradient: bfloat16 [65536, 512], P(('dp', 'ctx')), parts along dimension 0
- value_gradient: bfloat16 [65536, 512], P(('dp', 'ctx')), parts along dimension 0
The draws below stay inside these ranges and needn't reach their ends.
There are 32 independent parts, one for each index of `dp`. The reference program is written for one: setup_inputs(seed, part) draws one part's arguments, and reference() takes and returns one part's arrays. A program takes and returns all parts, laid end to end along the dimension named above; each array names one. Nothing has to cross between parts.
Inputs may be any that keep to these rules, and one draw needn't show every extreme that they name: `doc_blocks`: document numbers never fall along the blocks; every document covers 1 to 11 blocks and one covers exactly 11. `shard_order`: each shard number appears once; row shard i holds shard i or shard i + 1 - 2 * (i % 2), the other member of its pair.
All inputs are finite; a program needn't handle non-finite values.
Results may differ from the reference program's by a relative error of at most 0.035.
Values may be sent and summed in bfloat16 or wider, within the bound.
No kernel may reach another device: no remote copies, remote signals or barrier semaphores. Data moves between devices by JAX's collectives and lax.ppermute only.
A program may use at most 128 MiB of HBM per device.

```python
import math
import jax
import jax.numpy as jnp
import numpy as np
from jax import lax

QUERY_HEADS = 16
KEY_VALUE_HEADS = 4
HEAD_WIDTH = 128
BLOCK = 128
TOKENS_PER_PART = 128
QUERY_PER_KV = 4
PACKED_LENGTH = 2048
SHARDS = 16
BLOCKS = 16
MOST = 11
DOCS = 3
N_CTX = 16


def drawn_pair(key):
    base = jax.random.fold_in(key, 7)
    first_result, second_result = jax.random.split(base, 2)
    simple_key = jnp.clip(jax.random.normal(first_result, (PACKED_LENGTH, KEY_VALUE_HEADS, HEAD_WIDTH), jnp.float32), -6.0, 6.0)
    simple_query = jnp.clip(jax.random.normal(second_result, (PACKED_LENGTH, KEY_VALUE_HEADS, QUERY_PER_KV, HEAD_WIDTH), jnp.float32), -6.0, 6.0)
    key_rows = simple_key
    query_rows = simple_query
    return (query_rows.reshape(PACKED_LENGTH, QUERY_HEADS * HEAD_WIDTH), key_rows.reshape(PACKED_LENGTH, KEY_VALUE_HEADS * HEAD_WIDTH))


def draw_query(key, part):
    return drawn_pair(key)[0].astype(jnp.bfloat16)


def draw_key(key, part):
    return drawn_pair(key)[1].astype(jnp.bfloat16)


def draw_shard_order(key, part):
    flips = jax.random.randint(jax.random.fold_in(key, 3), (SHARDS // 2,), 0, 2, jnp.int32)
    base = jnp.arange(SHARDS, dtype=jnp.int32)
    return (base + (1 - 2 * (base % 2)) * jnp.repeat(flips, 2)).astype(jnp.int32)


def shard_levels(stream_key, shape, shards, least, top_value):
    def one(dim, parts):
        draws = jax.random.uniform(jax.random.fold_in(jax.random.fold_in(stream_key, 6), dim), (parts,), jnp.float32, least / len(shards), top_value / len(shards))
        return jnp.repeat(jnp.exp(draws), shape[dim] // parts).reshape((-1,) + (1,) * (len(shape) - dim - 1))

    loudness = one(*shards[0])
    for cut in shards[1:]:
        loudness = loudness * one(*cut)
    return loudness


def profile(number_of, total, limit, slope):
    weights = [(1 << 20) // math.isqrt(rank ** slope) + 1 for rank in range(2, number_of + 1)]
    surplus, given = total - limit - (number_of - 1), [1] * (number_of - 1)
    while surplus > 0:
        movable = [i for i in range(number_of - 1) if given[i] < limit]
        whole, left = sum([weights[i] for i in movable]), surplus
        for i in movable:
            addition = min(limit - given[i], max(1, left * weights[i] // whole), surplus)
            given[i] = given[i] + addition
            surplus = surplus - addition
    return np.array([limit] + given)


def uneven(key, count, total, most, slope):
    if count == 2:
        one = jax.random.randint(key, (), max(1, total - most), min(most, total - 1) + 1)
        return jnp.stack([one, total - one])
    lengths = jnp.asarray(profile(count, total, most, slope), jnp.int32)
    twos = (count - 1) // 2
    donor, sink = lengths[1:1 + 2 * twos:2], lengths[2:2 + 2 * twos:2]
    room = jnp.minimum(donor - 1, most - sink)
    moved = jax.random.randint(jax.random.fold_in(key, 1), (twos,), 0, 1 << 20) % (room + 1)
    lengths = lengths.at[1:1 + 2 * twos:2].set(donor - moved).at[2:2 + 2 * twos:2].set(sink + moved)
    return lengths[jax.random.permutation(jax.random.fold_in(key, 2), count)]


def gaussian(rng, extent, width, limit, cuts=(), held_as=jnp.bfloat16):
    entries = jax.random.normal(rng, extent, jnp.float32) * width
    if len(cuts) > 0:
        entries = shard_levels(rng, extent, cuts, -0.22, 0.18) * entries
    return jnp.clip(entries, min=-limit, max=limit).astype(held_as)


def setup_inputs(seed: int = 0, part: int = 0) -> dict:
    arg_keys = jax.random.split(jax.random.key(seed), 7)
    part_keys = jax.random.split(jax.random.fold_in(arg_keys[6], part), 7)
    return {
        "query": draw_query(jax.random.fold_in(jax.random.fold_in(arg_keys[6], part), 71), part),
        "key": draw_key(jax.random.fold_in(jax.random.fold_in(arg_keys[6], part), 71), part),
        "value": gaussian(part_keys[2], (PACKED_LENGTH, KEY_VALUE_HEADS * HEAD_WIDTH), 1.0, 6.0, ((0, 16),)),
        "output_gradient": gaussian(part_keys[3], (PACKED_LENGTH, QUERY_HEADS * HEAD_WIDTH), 1.0, 6.0, ((0, 16),)),
        "doc_blocks": jnp.searchsorted(jnp.cumsum(uneven(part_keys[4], DOCS, BLOCKS, MOST, 1)), jnp.arange(BLOCKS), side="right").astype(jnp.int32),
        "shard_order": draw_shard_order(jax.random.fold_in(jax.random.fold_in(arg_keys[6], part), 71), part),
    }


def reference(query, key, value, output_gradient, doc_blocks, shard_order):
    offsets = jnp.arange(TOKENS_PER_PART, dtype=jnp.int32)
    pos = (shard_order[:, None] * TOKENS_PER_PART + offsets[None, :]).reshape(PACKED_LENGTH).astype(jnp.int32)
    doc = doc_blocks[(pos // BLOCK).astype(jnp.int32)]
    allowed = (doc[:, None] == doc[None, :]) & (pos[None, :] <= pos[:, None])
    scale = HEAD_WIDTH ** -0.5
    query_rows = query.astype(jnp.float32).reshape(PACKED_LENGTH, KEY_VALUE_HEADS, QUERY_PER_KV, HEAD_WIDTH)
    key_rows = key.astype(jnp.float32).reshape(PACKED_LENGTH, KEY_VALUE_HEADS, HEAD_WIDTH)
    value_rows = value.astype(jnp.float32).reshape(PACKED_LENGTH, KEY_VALUE_HEADS, HEAD_WIDTH)
    gradient_list = output_gradient.astype(jnp.float32).reshape(PACKED_LENGTH, KEY_VALUE_HEADS, QUERY_PER_KV, HEAD_WIDTH)
    scores = jnp.einsum("qgjd,kgd->gjqk", query_rows, key_rows) * scale
    scores = jnp.where(allowed[None, None], scores, -jnp.inf)
    top = jnp.max(scores, axis=-1, keepdims=True)
    lse = top + jnp.log(jnp.sum(jnp.exp(scores - top), axis=-1, keepdims=True))
    attention_weights = lax.optimization_barrier(jnp.exp(scores - lse).astype(jnp.bfloat16)).astype(jnp.float32)
    attn = jnp.einsum("gjqk,kgd->qgjd", attention_weights, value_rows).astype(jnp.bfloat16)
    delta = jnp.transpose(jnp.sum(gradient_list * attn.astype(jnp.float32), axis=-1), (1, 2, 0))
    dprob = jnp.einsum("qgjd,kgd->gjqk", gradient_list, value_rows)
    score_gradient = lax.optimization_barrier((attention_weights * (dprob - delta[..., None])).astype(jnp.bfloat16)).astype(jnp.float32)
    grad_query = (jnp.einsum("gjqk,kgd->qgjd", score_gradient, key_rows) * scale).astype(jnp.bfloat16)
    score_grad_split = score_gradient.reshape(KEY_VALUE_HEADS, QUERY_PER_KV, N_CTX, TOKENS_PER_PART, PACKED_LENGTH)
    weight_split_rows = attention_weights.reshape(KEY_VALUE_HEADS, QUERY_PER_KV, N_CTX, TOKENS_PER_PART, PACKED_LENGTH)
    query_split_rows = query_rows.reshape(N_CTX, TOKENS_PER_PART, KEY_VALUE_HEADS, QUERY_PER_KV, HEAD_WIDTH)
    output_grad_split = gradient_list.reshape(N_CTX, TOKENS_PER_PART, KEY_VALUE_HEADS, QUERY_PER_KV, HEAD_WIDTH)
    key_pieces_list = jnp.einsum("gjnqk,nqgjd->nkgd", score_grad_split, query_split_rows) * scale
    value_pieces_list = jnp.einsum("gjnqk,nqgjd->nkgd", weight_split_rows, output_grad_split)
    key_pieces_list = lax.optimization_barrier(key_pieces_list.astype(jnp.bfloat16)).astype(jnp.float32)
    value_pieces_list = lax.optimization_barrier(value_pieces_list.astype(jnp.bfloat16)).astype(jnp.float32)
    key_gradient = jnp.sum(key_pieces_list, axis=0).astype(jnp.bfloat16).reshape(PACKED_LENGTH, KEY_VALUE_HEADS * HEAD_WIDTH)
    value_gradient = jnp.sum(value_pieces_list, axis=0).astype(jnp.bfloat16).reshape(PACKED_LENGTH, KEY_VALUE_HEADS * HEAD_WIDTH)
    return (attn.reshape(PACKED_LENGTH, QUERY_HEADS * HEAD_WIDTH), grad_query.reshape(PACKED_LENGTH, QUERY_HEADS * HEAD_WIDTH), key_gradient, value_gradient)
```

```python
import jax
import jax.numpy as jnp
from jax import lax
from jax.experimental import pallas as pl
from jax.experimental.pallas import tpu as pltpu
from jax.sharding import PartitionSpec as P

GROUPS = 4
PER = 4
D = 128
T = 128
UNIT = 256
MAXU = 6
BLOCKS = 16
SCALE = D ** -0.5
LOG2E = 1.4426950408889634
FAR = 1 << 24


def nt(a, b):
    return lax.dot_general(a, b, (((1,), (1,)), ((), ())), preferred_element_type=jnp.float32)


def tn(a, b):
    return lax.dot_general(a, b, (((0,), (0,)), ((), ())), preferred_element_type=jnp.float32)


def nn(a, b):
    return lax.dot_general(a, b, (((1,), (0,)), ((), ())), preferred_element_type=jnp.float32)


def kernel(docs, order, place, q_ref, do_ref, k_ref, v_ref, o_ref, dq_ref, dkv_ref, e_buf):
    rows = PER * T
    own = order[place[0]]
    own_doc = docs[own]
    first = sum((docs[b] < own_doc).astype(jnp.int32) for b in range(BLOCKS)) >> 1
    count = (own >> 1) - first + 1
    base = own * T

    def start_of(row):
        s = order[row]
        return jnp.where(docs[s] == own_doc, s * T, FAR)

    q = jnp.concatenate([q_ref[:, j * D:(j + 1) * D] for j in range(PER)], axis=0)
    do = jnp.concatenate([do_ref[:, j * D:(j + 1) * D] for j in range(PER)], axis=0)
    do_t = do.astype(jnp.float32).T
    q_pos = base + lax.rem(lax.broadcasted_iota(jnp.int32, (1, rows), 1), T)
    half = lax.broadcasted_iota(jnp.int32, (UNIT, 1), 0)

    def fold_max(a):
        return jnp.max(a.reshape(UNIT // 8, 8, rows), axis=0)

    def fold_sum(a):
        return jnp.sum(a.reshape(UNIT // 8, 8, rows), axis=0)

    def score(i, top):
        u = first + i
        at = pl.multiple_of(u * UNIT, UNIT)
        s = nt(k_ref[pl.ds(at, UNIT), :], q)
        k_pos = jnp.where(half < T, start_of(2 * u) + half, start_of(2 * u + 1) + half - T)
        s = jnp.where(k_pos <= q_pos, s, -jnp.inf)
        e_buf[pl.ds(pl.multiple_of(i * UNIT, UNIT), UNIT), :] = s
        return jnp.maximum(top, fold_max(s))

    top8 = lax.fori_loop(0, count, score, jnp.full((8, rows), -jnp.inf, jnp.float32))
    top = jnp.max(top8, axis=0, keepdims=True)

    def weigh(i, carry):
        total, out_t = carry
        at = pl.multiple_of((first + i) * UNIT, UNIT)
        sl = pl.ds(pl.multiple_of(i * UNIT, UNIT), UNIT)
        e = jnp.exp2((e_buf[sl, :] - top) * (SCALE * LOG2E))
        e_buf[sl, :] = e
        v = v_ref[pl.ds(at, UNIT), :]
        return total + fold_sum(e), out_t + tn(v, e.astype(jnp.bfloat16))

    total8, out_t = lax.fori_loop(
        0, count, weigh, (jnp.zeros((8, rows), jnp.float32), jnp.zeros((D, rows), jnp.float32))
    )
    inv = 1.0 / jnp.sum(total8, axis=0, keepdims=True)
    attn_t = (out_t * inv).astype(jnp.bfloat16).astype(jnp.float32)
    delta = jnp.sum(attn_t * do_t, axis=0, keepdims=True)
    for j in range(PER):
        o_ref[:, j * D:(j + 1) * D] = attn_t[:, j * T:(j + 1) * T].T.astype(jnp.bfloat16)

    dkv_ref[...] = jnp.zeros_like(dkv_ref)

    def back(i, dq_t):
        at = pl.multiple_of((first + i) * UNIT, UNIT)
        sl = pl.ds(pl.multiple_of(i * UNIT, UNIT), UNIT)
        k = k_ref[pl.ds(at, UNIT), :]
        v = v_ref[pl.ds(at, UNIT), :]
        w = e_buf[sl, :] * inv
        dp = nt(v, do)
        ds = (w * (dp - delta)).astype(jnp.bfloat16)
        dkv_ref[pl.ds(at, UNIT), :D] = (nn(ds, q) * SCALE).astype(jnp.bfloat16)
        dkv_ref[pl.ds(at, UNIT), D:] = nn(w.astype(jnp.bfloat16), do).astype(jnp.bfloat16)
        return dq_t + tn(k, ds)

    dq_t = lax.fori_loop(0, count, back, jnp.zeros((D, rows), jnp.float32)) * SCALE
    for j in range(PER):
        dq_ref[:, j * D:(j + 1) * D] = dq_t[:, j * T:(j + 1) * T].T.astype(jnp.bfloat16)


def shards(query, key, value, output_gradient, doc_blocks, shard_order):
    me = lax.axis_index("ctx")
    kv = jnp.concatenate((key, value), axis=1)
    kv_all = lax.all_gather(kv, "ctx", axis=0, tiled=True)
    tokens = kv_all.shape[0]
    attn, grad_query, dkv = pl.pallas_call(
        kernel,
        grid_spec=pltpu.PrefetchScalarGridSpec(
            num_scalar_prefetch=3,
            grid=(GROUPS,),
            in_specs=[
                pl.BlockSpec((T, PER * D), lambda g, *_: (0, g)),
                pl.BlockSpec((T, PER * D), lambda g, *_: (0, g)),
                pl.BlockSpec((tokens, D), lambda g, *_: (0, g)),
                pl.BlockSpec((tokens, D), lambda g, *_: (0, GROUPS + g)),
            ],
            out_specs=[
                pl.BlockSpec((T, PER * D), lambda g, *_: (0, g)),
                pl.BlockSpec((T, PER * D), lambda g, *_: (0, g)),
                pl.BlockSpec((tokens, 2 * D), lambda g, *_: (0, g)),
            ],
            scratch_shapes=[pltpu.VMEM((MAXU * UNIT, PER * T), jnp.float32)],
        ),
        out_shape=[
            jax.ShapeDtypeStruct(query.shape, jnp.bfloat16),
            jax.ShapeDtypeStruct(query.shape, jnp.bfloat16),
            jax.ShapeDtypeStruct((tokens, 2 * GROUPS * D), jnp.bfloat16),
        ],
        compiler_params=pltpu.CompilerParams(
            dimension_semantics=("arbitrary",), vmem_limit_bytes=56 * 1024 * 1024
        ),
        name="attention",
    )(doc_blocks, shard_order, me.reshape(1), query, output_gradient, kv_all, kv_all)
    grads = lax.psum_scatter(dkv, "ctx", scatter_dimension=0, tiled=True)
    return (
        attn,
        grad_query,
        jnp.concatenate([grads[:, 2 * D * g:2 * D * g + D] for g in range(GROUPS)], axis=1),
        jnp.concatenate([grads[:, 2 * D * g + D:2 * D * g + 2 * D] for g in range(GROUPS)], axis=1),
    )


def solution(mesh):
    rows = P(("dp", "ctx"), None)
    return jax.shard_map(
        shards,
        mesh=mesh,
        in_specs=(rows, rows, rows, rows, P("dp"), P("dp")),
        out_specs=(rows, rows, rows, rows),
        check_vma=False,
    )
```

```python
import functools

import jax
import jax.numpy as jnp
from jax import lax
from jax.experimental import pallas as pl
from jax.experimental.pallas import tpu as pltpu
from jax.sharding import PartitionSpec as P

D = 128
T = 128
UNIT = 256
ROWS = 512
CHUNKS = 4
HALF_Q = 1024
HALF_KV = 256
CHIPS = 8
SCALE = D ** -0.5
FACTOR = SCALE * 1.4426950408889634
INF = float("inf")


def nt(a, b):
    return lax.dot_general(a, b, (((1,), (1,)), ((), ())), preferred_element_type=jnp.float32)


def tn(a, b):
    return lax.dot_general(a, b, (((0,), (0,)), ((), ())), preferred_element_type=jnp.float32)


def nn(a, b):
    return lax.dot_general(a, b, (((1,), (0,)), ((), ())), preferred_element_type=jnp.float32)


def fold_max(a):
    return jnp.max(a.reshape(a.shape[0] // 8, 8, a.shape[1]), axis=0)


def fold_sum(a):
    return jnp.sum(a.reshape(a.shape[0] // 8, 8, a.shape[1]), axis=0)


def dead_terms(docs, order, me, distance):
    there = jnp.maximum(me - 2 * distance, me & 1)
    keys = (order[there], order[there ^ 1])
    queries = (order[me], order[me ^ 1])
    near = me >= 2 * distance

    def meets(k, q):
        return near & (docs[k] == docs[q]) & (k <= q)

    table = [[meets(k, q) for k in keys] for q in queries]
    alive = table[0][0] | table[0][1] | table[1][0] | table[1][1]
    return [[jnp.where(m, 0.0, INF) for m in row] for row in table], alive


def columns(h, base=0):
    return pl.ds(pl.multiple_of(base + h * D, D), D)


def causal():
    k = lax.broadcasted_iota(jnp.int32, (T, ROWS), 0)
    q = lax.rem(lax.broadcasted_iota(jnp.int32, (T, ROWS), 1), T)
    return k <= q


def both(a, b):
    return jnp.concatenate([a, b], axis=0)


def forward_unit(u_ref, q_ref, m_ref, l_ref, acc_ref, dead):
    def head(h, _):
        k, v = u_ref[:, columns(h)], u_ref[:, columns(h, HALF_KV)]
        for half in range(2):
            chunk = 2 * h + half
            s = nt(k, q_ref[chunk])
            d0, d1 = dead[half]
            peak = jnp.maximum(fold_max(s[:T]) - d0, fold_max(s[T:]) - d1)
            old = m_ref[chunk]
            new = jnp.maximum(old, jnp.max(peak, axis=0, keepdims=True))
            m_ref[chunk] = new
            fade = jnp.exp2((old - new) * FACTOR)
            shift = new[:1] * FACTOR
            e0 = jnp.exp2(s[:T] * FACTOR - (shift + d0))
            e1 = jnp.exp2(s[T:] * FACTOR - (shift + d1))
            l_ref[chunk] = l_ref[chunk] * fade + fold_sum(e0) + fold_sum(e1)
            acc_ref[chunk] = acc_ref[chunk] * fade[:1] + tn(v, both(e0, e1).astype(jnp.bfloat16))
        return 0

    lax.fori_loop(0, 2, head, 0, unroll=True)


def backward_unit(u_ref, q_ref, do_ref, lse_ref, delta_ref, dq_ref, g_ref, dead, own):
    def head(h, _):
        k, v = u_ref[:, columns(h)], u_ref[:, columns(h, HALF_KV)]
        dk = dv = None
        for half in range(2):
            chunk = 2 * h + half
            q, do = q_ref[chunk], do_ref[chunk]
            s = nt(k, q)
            shift, delta = lse_ref[chunk][:1], delta_ref[chunk][:1]
            w = [jnp.exp2(s[T * i:T * i + T] * FACTOR - (shift + dead[half][i])) for i in range(2)]
            if own:
                w[half] = jnp.where(causal(), w[half], 0.0)
            w = both(*w)
            ds = (w * (nt(v, do) - delta)).astype(jnp.bfloat16)
            k_term = nn(ds, q)
            v_term = nn(w.astype(jnp.bfloat16), do)
            dk = k_term if dk is None else dk + k_term
            dv = v_term if dv is None else dv + v_term
            dq_ref[chunk] += tn(k, ds)
        g_ref[:, columns(h)] = (dk * SCALE).astype(jnp.bfloat16)
        g_ref[:, columns(h, HALF_KV)] = dv.astype(jnp.bfloat16)
        return 0

    lax.fori_loop(0, 2, head, 0, unroll=True)


def first_kernel(docs, order, place, q_own, do_own, other, u_ref, q_ref, do_ref, m_ref, l_ref, acc_ref):
    me = place[0]
    dead, _ = dead_terms(docs, order, me, 0)
    sides = ((q_own, do_own), (other.at[:, :HALF_Q], other.at[:, HALF_Q:2 * HALF_Q]))

    for h in range(2):
        k, v = u_ref[:, h * D:(h + 1) * D], u_ref[:, HALF_KV + h * D:HALF_KV + (h + 1) * D]
        for half in range(2):
            chunk = 2 * h + half
            for source, target in zip(sides[half], (q_ref, do_ref)):
                for j in range(4):
                    target[chunk, j * T:(j + 1) * T, :] = source[:, (4 * h + j) * D:(4 * h + j + 1) * D]
            s = nt(k, q_ref[chunk])
            part = [s[:T], s[T:]]
            part[half] = jnp.where(causal(), part[half], -INF)
            part[1 - half] = part[1 - half] - dead[half][1 - half]
            s = both(*part)
            top = jnp.max(fold_max(s), axis=0, keepdims=True)
            e = jnp.exp2((s - top) * FACTOR)
            m_ref[chunk] = jnp.broadcast_to(top, (8, ROWS))
            l_ref[chunk] = fold_sum(e)
            acc_ref[chunk] = tn(v, e.astype(jnp.bfloat16))


def near_kernel(units, docs, order, place, q_ref, m_in, l_in, acc_in, *refs):
    n = len(units)
    m_ref, l_ref, acc_ref = refs[n:]
    m_ref[...] = m_in[...]
    l_ref[...] = l_in[...]
    acc_ref[...] = acc_in[...]
    forward_units(units, refs[:n], docs, order, place[0], q_ref, m_ref, l_ref, acc_ref)


def forward_units(units, u_refs, docs, order, me, q_ref, m_ref, l_ref, acc_ref):
    for distance, u_ref in zip(units, u_refs):
        dead, alive = dead_terms(docs, order, me, distance)

        @pl.when(alive)
        def _():
            forward_unit(u_ref, q_ref, m_ref, l_ref, acc_ref, dead)


def middle_kernel(docs, order, place, q_ref, do_ref, m_in, l_in, acc_in, u3, u4, o_own, o_send, lse_ref, delta_ref, dq_ref, g3, g4, m_ref, l_ref, acc_ref):
    me = place[0]
    m_ref[...] = m_in[...]
    l_ref[...] = l_in[...]
    acc_ref[...] = acc_in[...]
    forward_units((3, 4), (u3, u4), docs, order, me, q_ref, m_ref, l_ref, acc_ref)
    for chunk in range(CHUNKS):
        total = jnp.sum(l_ref[chunk], axis=0, keepdims=True)
        attn = (acc_ref[chunk] * (1.0 / total)).astype(jnp.bfloat16).astype(jnp.float32)
        do_t = do_ref[chunk].astype(jnp.float32).T
        lse_ref[chunk] = m_ref[chunk] * FACTOR + jnp.log2(total)
        delta_ref[chunk] = jnp.broadcast_to(jnp.sum(attn * do_t, axis=0, keepdims=True), (8, ROWS))
        out = (o_own, o_send)[chunk % 2]
        for j in range(4):
            at = (chunk // 2 * 4 + j) * D
            out[:, at:at + D] = attn[:, j * T:(j + 1) * T].T.astype(jnp.bfloat16)
    dq_ref[...] = jnp.zeros_like(dq_ref)
    backward_units((4, 3), (u4, u3), (g4, g3), docs, order, me, q_ref, do_ref, lse_ref, delta_ref, dq_ref)


def backward_units(units, u_refs, g_refs, docs, order, me, q_ref, do_ref, lse_ref, delta_ref, dq_ref):
    for distance, u_ref, g_ref in zip(units, u_refs, g_refs):
        dead, alive = dead_terms(docs, order, me, distance)

        @pl.when(alive)
        def _():
            backward_unit(u_ref, q_ref, do_ref, lse_ref, delta_ref, dq_ref, g_ref, dead, distance == 0)

        if distance > 0:
            @pl.when(jnp.logical_not(alive))
            def _():
                g_ref[...] = jnp.zeros_like(g_ref)


def back_kernel(units, docs, order, place, *refs):
    q_ref, do_ref, lse_ref, delta_ref, dq_in = refs[:5]
    n = len(units)
    final = 0 in units
    u_refs, outs = refs[5:5 + n], refs[5 + n + final:]
    g_refs = outs[:n]
    dq_ref = outs[-1]
    me = place[0]
    dq_ref[...] = dq_in[...]
    backward_units(units, u_refs, g_refs, docs, order, me, q_ref, do_ref, lse_ref, delta_ref, dq_ref)
    if final:
        o_send, packed = refs[5 + n], outs[n + 1]
        packed[:, :HALF_Q] = o_send[...]
        for chunk in range(CHUNKS):
            dq = dq_ref[chunk] * SCALE
            for j in range(4):
                at = (chunk // 2 * 4 + j) * D
                tile = dq[:, j * T:(j + 1) * T].T.astype(jnp.bfloat16)
                if chunk % 2 == 0:
                    outs[n][:, at:at + D] = tile
                else:
                    packed[:, HALF_Q + at:HALF_Q + at + D] = tile


def call(body, name, scalars, operands, specs, outs, scratch=()):
    whole = lambda shape: pl.BlockSpec(shape, lambda i, *_: (0,) * len(shape))
    return pl.pallas_call(
        body,
        grid_spec=pltpu.PrefetchScalarGridSpec(
            num_scalar_prefetch=3,
            grid=(1,),
            in_specs=[whole(a.shape) if s is None else s for a, s in zip(operands, specs)],
            out_specs=[whole(o.shape) for o in outs],
            scratch_shapes=list(scratch),
        ),
        out_shape=list(outs),
        cost_estimate=pl.CostEstimate(flops=1024, bytes_accessed=1024, transcendentals=0),
        compiler_params=pltpu.CompilerParams(
            dimension_semantics=("arbitrary",), vmem_limit_bytes=40 * 1024 * 1024
        ),
        name=name,
    )(*scalars, *operands)


def hop(x, pairs, cross=0):
    return lax.ppermute(x, "ctx", [(2 * a + c, 2 * b + (c ^ cross)) for a, b in pairs for c in range(2)])


def after(x, *others):
    return lax.optimization_barrier((x,) + others)[0]


def swap(x):
    return lax.ppermute(x, "ctx", [(i, i ^ 1) for i in range(2 * CHIPS)])


def struct(shape, dtype=jnp.float32):
    return jax.ShapeDtypeStruct(shape, dtype)


def shards(query, key, value, output_gradient, doc_blocks, shard_order):
    me = lax.axis_index("ctx")
    core = me & 1
    scalars = (doc_blocks, shard_order, me.reshape(1))

    def side(x, which, width):
        return lax.dynamic_slice_in_dim(x, which * width, width, axis=1)

    kv_own = jnp.concatenate((side(key, core, HALF_KV), side(value, core, HALF_KV)), axis=1)
    across = swap(jnp.concatenate(
        (side(query, 1 - core, HALF_Q), side(output_gradient, 1 - core, HALF_Q), side(key, 1 - core, HALF_KV), side(value, 1 - core, HALF_KV)),
        axis=1,
    ))
    u0 = jnp.concatenate((kv_own, across[:, 2 * HALF_Q:]), axis=0)
    u6 = hop(u0, [(s, (s + 6) % CHIPS) for s in range(4)])
    u1 = hop(u0, [(s, s + 1) for s in range(7)])
    u5 = hop(u6, [((s + 6) % CHIPS, (s + 5) % CHIPS) for s in range(4)])
    u2 = hop(u1, [(s, s + 1) for s in range(1, 7)])
    u3 = hop(u2, [(s, s + 1) for s in range(2, 7)])
    u4 = hop(u5, [(s, (s - 1) % CHIPS) for s in (5, 6, 7, 0)])

    mine = pl.BlockSpec((T, HALF_Q), lambda i, d, o, p: (0, p[0] & 1))
    stats = struct((CHUNKS, 8, ROWS))
    wide = struct((CHUNKS, D, ROWS))
    stacked = struct((CHUNKS, ROWS, D), jnp.bfloat16)
    unit = struct((UNIT, 2 * HALF_KV), jnp.bfloat16)
    packed = struct((T, 2 * HALF_Q), jnp.bfloat16)
    token_half = struct((T, HALF_Q), jnp.bfloat16)
    held = [pltpu.VMEM(x.shape, x.dtype) for x in (stats, stats, wide)]

    q, do, m0, l0, acc0 = call(
        first_kernel, "own", scalars, (query, output_gradient, across, u0),
        (mine, mine, None, None), (stacked, stacked, stats, stats, wide),
    )
    m1, l1, acc1 = call(
        functools.partial(near_kernel, (1, 2)), "near", scalars, (q, m0, l0, acc0, u1, u2), (None,) * 6,
        (stats, stats, wide),
    )
    m2, l2, acc2 = call(
        functools.partial(near_kernel, (5,)), "far", scalars, (q, m1, l1, acc1, u5), (None,) * 5,
        (stats, stats, wide),
    )
    o_own, o_send, lse, delta, dq3, g3, g4 = call(
        middle_kernel, "middle", scalars, (q, do, m2, l2, acc2, u3, u4), (None,) * 7,
        (token_half, token_half, stats, stats, wide, unit, unit), held,
    )

    def back(units, name, dq, held_units):
        n = len(units)
        outs = (unit,) * n + ((token_half, packed) if 0 in units else (wide,))
        return call(
            functools.partial(back_kernel, units), name, scalars, (q, do, lse, delta, dq, *held_units),
            (None,) * (5 + len(held_units)), outs, held[2:] if 0 in units else (),
        )

    def add(*terms):
        total = terms[0].astype(jnp.float32)
        for term in terms[1:]:
            total = total + term.astype(jnp.float32)
        return total.astype(jnp.bfloat16)

    b4 = hop(g4, [(t, (t + 1) % CHIPS) for t in range(4, 8)])
    b3 = hop(g3, [(t, t - 1) for t in range(3, 8)])
    g5, g2, dq2 = back((5, 2), "back52", dq3, (u5, u2))
    a5 = add(g5, b4)
    a2 = add(g2, b3)
    r5 = hop(a5, [(t, (t + 3) % CHIPS) for t in (5, 6, 7, 0)])
    b2 = hop(a2, [(t, t - 1) for t in range(2, 8)])
    g1, g0, dq_own, sent = back((1, 0), "back10", after(dq2, a5, a2), (u1, u0, o_send))
    a1 = add(g1, b2)
    r1 = [hop(a1[i * T:(i + 1) * T], [(t, t - 1) for t in range(1, 8)], i) for i in range(2)]
    other = swap(sent)
    s05 = add(g0, r5)
    s05_other = swap(s05[T:])

    def join(own, other):
        return jnp.where(core == 0, jnp.concatenate((own, other), axis=1), jnp.concatenate((other, own), axis=1))

    sums = add(s05[:T], r1[0])
    sums_other = add(s05_other, r1[1])
    return (
        join(o_own, other[:, :HALF_Q]),
        join(dq_own, other[:, HALF_Q:2 * HALF_Q]),
        join(sums[:, :HALF_KV], sums_other[:, :HALF_KV]),
        join(sums[:, HALF_KV:], sums_other[:, HALF_KV:]),
    )


def solution(mesh):
    rows = P(("dp", "ctx"), None)
    return jax.shard_map(
        shards,
        mesh=mesh,
        in_specs=(rows, rows, rows, rows, P("dp"), P("dp")),
        out_specs=(rows, rows, rows, rows),
        check_vma=False,
    )
```

```python
import functools

import jax
import jax.numpy as jnp
from jax import lax
from jax.experimental import pallas as pl
from jax.experimental.pallas import tpu as pltpu
from jax.sharding import PartitionSpec as P

D = 128
T = 128
UNIT = 256
ROWS = 512
CHUNKS = 4
HALF_Q = 1024
HALF_KV = 256
CHIPS = 8
SCALE = D ** -0.5
FACTOR = SCALE * 1.4426950408889634
INF = float("inf")


def nt(a, b):
    return lax.dot_general(a, b, (((1,), (1,)), ((), ())), preferred_element_type=jnp.float32)


def tn(a, b):
    return lax.dot_general(a, b, (((0,), (0,)), ((), ())), preferred_element_type=jnp.float32)


def nn(a, b):
    return lax.dot_general(a, b, (((1,), (0,)), ((), ())), preferred_element_type=jnp.float32)


def fold_max(a):
    return jnp.max(a.reshape(a.shape[0] // 8, 8, a.shape[1]), axis=0)


def fold_sum(a):
    return jnp.sum(a.reshape(a.shape[0] // 8, 8, a.shape[1]), axis=0)


def dead_terms(docs, order, me, distance):
    there = jnp.maximum(me - 2 * distance, me & 1)
    keys = (order[there], order[there ^ 1])
    queries = (order[me], order[me ^ 1])
    near = me >= 2 * distance

    def meets(k, q):
        return near & (docs[k] == docs[q]) & (k <= q)

    table = [[meets(k, q) for k in keys] for q in queries]
    alive = table[0][0] | table[0][1] | table[1][0] | table[1][1]
    return [[jnp.where(m, 0.0, INF) for m in row] for row in table], alive


def columns(h, base=0):
    return pl.ds(pl.multiple_of(base + h * D, D), D)


def causal():
    k = lax.broadcasted_iota(jnp.int32, (T, ROWS), 0)
    q = lax.rem(lax.broadcasted_iota(jnp.int32, (T, ROWS), 1), T)
    return k <= q


def both(a, b):
    return jnp.concatenate([a, b], axis=0)


def forward_unit(u_ref, q_ref, m_ref, l_ref, acc_ref, dead):
    def head(h, _):
        k, v = u_ref[:, columns(h)], u_ref[:, columns(h, HALF_KV)]
        for half in range(2):
            chunk = 2 * h + half
            s = nt(k, q_ref[chunk])
            d0, d1 = dead[half]
            peak = jnp.maximum(fold_max(s[:T]) - d0, fold_max(s[T:]) - d1)
            old = m_ref[chunk]
            new = jnp.maximum(old, jnp.max(peak, axis=0, keepdims=True))
            m_ref[chunk] = new
            fade = jnp.exp2((old - new) * FACTOR)
            shift = new[:1] * FACTOR
            e0 = jnp.exp2(s[:T] * FACTOR - (shift + d0))
            e1 = jnp.exp2(s[T:] * FACTOR - (shift + d1))
            l_ref[chunk] = l_ref[chunk] * fade + fold_sum(e0) + fold_sum(e1)
            acc_ref[chunk] = acc_ref[chunk] * fade[:1] + tn(v, both(e0, e1).astype(jnp.bfloat16))
        return 0

    lax.fori_loop(0, 2, head, 0, unroll=True)


def backward_unit(u_ref, q_ref, do_ref, lse_ref, delta_ref, dq_ref, g_ref, dead, own):
    def head(h, _):
        k, v = u_ref[:, columns(h)], u_ref[:, columns(h, HALF_KV)]
        dk = dv = None
        for half in range(2):
            chunk = 2 * h + half
            q, do = q_ref[chunk], do_ref[chunk]
            s = nt(k, q)
            shift, delta = lse_ref[chunk][:1], delta_ref[chunk][:1]
            w = [jnp.exp2(s[T * i:T * i + T] * FACTOR - (shift + dead[half][i])) for i in range(2)]
            if own:
                w[half] = jnp.where(causal(), w[half], 0.0)
            w = both(*w)
            ds = (w * (nt(v, do) - delta)).astype(jnp.bfloat16)
            k_term = nn(ds, q)
            v_term = nn(w.astype(jnp.bfloat16), do)
            dk = k_term if dk is None else dk + k_term
            dv = v_term if dv is None else dv + v_term
            dq_ref[chunk] += tn(k, ds)
        g_ref[:, columns(h)] = (dk * SCALE).astype(jnp.bfloat16)
        g_ref[:, columns(h, HALF_KV)] = dv.astype(jnp.bfloat16)
        return 0

    lax.fori_loop(0, 2, head, 0, unroll=True)


def first_kernel(docs, order, place, q_own, do_own, other, u_ref, q_ref, do_ref, m_ref, l_ref, acc_ref):
    me = place[0]
    dead, _ = dead_terms(docs, order, me, 0)
    sides = ((q_own, do_own), (other.at[:, :HALF_Q], other.at[:, HALF_Q:2 * HALF_Q]))

    for h in range(2):
        k, v = u_ref[:, h * D:(h + 1) * D], u_ref[:, HALF_KV + h * D:HALF_KV + (h + 1) * D]
        for half in range(2):
            chunk = 2 * h + half
            for source, target in zip(sides[half], (q_ref, do_ref)):
                for j in range(4):
                    target[chunk, j * T:(j + 1) * T, :] = source[:, (4 * h + j) * D:(4 * h + j + 1) * D]
            s = nt(k, q_ref[chunk])
            part = [s[:T], s[T:]]
            part[half] = jnp.where(causal(), part[half], -INF)
            part[1 - half] = part[1 - half] - dead[half][1 - half]
            s = both(*part)
            top = jnp.max(fold_max(s), axis=0, keepdims=True)
            e = jnp.exp2((s - top) * FACTOR)
            m_ref[chunk] = jnp.broadcast_to(top, (8, ROWS))
            l_ref[chunk] = fold_sum(e)
            acc_ref[chunk] = tn(v, e.astype(jnp.bfloat16))


def near_kernel(units, docs, order, place, q_ref, m_in, l_in, acc_in, *refs):
    n = len(units)
    m_ref, l_ref, acc_ref = refs[n:]
    m_ref[...] = m_in[...]
    l_ref[...] = l_in[...]
    acc_ref[...] = acc_in[...]
    forward_units(units, refs[:n], docs, order, place[0], q_ref, m_ref, l_ref, acc_ref)


def forward_units(units, u_refs, docs, order, me, q_ref, m_ref, l_ref, acc_ref):
    for distance, u_ref in zip(units, u_refs):
        dead, alive = dead_terms(docs, order, me, distance)

        @pl.when(alive)
        def _():
            forward_unit(u_ref, q_ref, m_ref, l_ref, acc_ref, dead)


def middle_kernel(docs, order, place, q_ref, do_ref, m_in, l_in, acc_in, u3, u4, o_own, o_send, lse_ref, delta_ref, dq_ref, g3, g4, m_ref, l_ref, acc_ref):
    me = place[0]
    m_ref[...] = m_in[...]
    l_ref[...] = l_in[...]
    acc_ref[...] = acc_in[...]
    forward_units((4,), (u4,), docs, order, me, q_ref, m_ref, l_ref, acc_ref)
    for chunk in range(CHUNKS):
        total = jnp.sum(l_ref[chunk], axis=0, keepdims=True)
        attn = (acc_ref[chunk] * (1.0 / total)).astype(jnp.bfloat16).astype(jnp.float32)
        do_t = do_ref[chunk].astype(jnp.float32).T
        lse_ref[chunk] = m_ref[chunk] * FACTOR + jnp.log2(total)
        delta_ref[chunk] = jnp.broadcast_to(jnp.sum(attn * do_t, axis=0, keepdims=True), (8, ROWS))
        out = (o_own, o_send)[chunk % 2]
        for j in range(4):
            at = (chunk // 2 * 4 + j) * D
            out[:, at:at + D] = attn[:, j * T:(j + 1) * T].T.astype(jnp.bfloat16)
    dq_ref[...] = jnp.zeros_like(dq_ref)
    backward_units((4, 3), (u4, u3), (g4, g3), docs, order, me, q_ref, do_ref, lse_ref, delta_ref, dq_ref)


def backward_units(units, u_refs, g_refs, docs, order, me, q_ref, do_ref, lse_ref, delta_ref, dq_ref):
    for distance, u_ref, g_ref in zip(units, u_refs, g_refs):
        dead, alive = dead_terms(docs, order, me, distance)

        @pl.when(alive)
        def _():
            backward_unit(u_ref, q_ref, do_ref, lse_ref, delta_ref, dq_ref, g_ref, dead, distance == 0)

        if distance > 0:
            @pl.when(jnp.logical_not(alive))
            def _():
                g_ref[...] = jnp.zeros_like(g_ref)


def back_kernel(units, docs, order, place, *refs):
    q_ref, do_ref, lse_ref, delta_ref, dq_in = refs[:5]
    n = len(units)
    final = 0 in units
    u_refs, outs = refs[5:5 + n], refs[5 + n + final:]
    g_refs = outs[:n]
    dq_ref = outs[-1]
    me = place[0]
    dq_ref[...] = dq_in[...]
    backward_units(units, u_refs, g_refs, docs, order, me, q_ref, do_ref, lse_ref, delta_ref, dq_ref)
    if final:
        o_send, packed = refs[5 + n], outs[n + 1]
        packed[:, :HALF_Q] = o_send[...]
        for chunk in range(CHUNKS):
            dq = dq_ref[chunk] * SCALE
            for j in range(4):
                at = (chunk // 2 * 4 + j) * D
                tile = dq[:, j * T:(j + 1) * T].T.astype(jnp.bfloat16)
                if chunk % 2 == 0:
                    outs[n][:, at:at + D] = tile
                else:
                    packed[:, HALF_Q + at:HALF_Q + at + D] = tile


def sum_kernel(docs, order, place, a_ref, b_ref, out_ref):
    out_ref[...] = (a_ref[...].astype(jnp.float32) + b_ref[...].astype(jnp.float32)).astype(jnp.bfloat16)


def call(body, name, scalars, operands, specs, outs, scratch=(), flops=1024):
    whole = lambda shape: pl.BlockSpec(shape, lambda i, *_: (0,) * len(shape))
    return pl.pallas_call(
        body,
        grid_spec=pltpu.PrefetchScalarGridSpec(
            num_scalar_prefetch=3,
            grid=(1,),
            in_specs=[whole(a.shape) if s is None else s for a, s in zip(operands, specs)],
            out_specs=[whole(o.shape) for o in outs],
            scratch_shapes=list(scratch),
        ),
        out_shape=list(outs),
        cost_estimate=pl.CostEstimate(flops=flops, bytes_accessed=1024, transcendentals=0),
        compiler_params=pltpu.CompilerParams(
            dimension_semantics=("arbitrary",), vmem_limit_bytes=40 * 1024 * 1024
        ),
        name=name,
    )(*scalars, *operands)


def hop(x, pairs, cross=0):
    return lax.ppermute(x, "ctx", [(2 * a + c, 2 * b + (c ^ cross)) for a, b in pairs for c in range(2)])


def after(x, *others):
    return lax.optimization_barrier((x,) + others)[0]


def swap(x):
    return lax.ppermute(x, "ctx", [(i, i ^ 1) for i in range(2 * CHIPS)])


def struct(shape, dtype=jnp.float32):
    return jax.ShapeDtypeStruct(shape, dtype)


def shards(query, key, value, output_gradient, doc_blocks, shard_order):
    me = lax.axis_index("ctx")
    core = me & 1
    scalars = (doc_blocks, shard_order, me.reshape(1))

    def side(x, which, width):
        return lax.dynamic_slice_in_dim(x, which * width, width, axis=1)

    kv_own = jnp.concatenate((side(key, core, HALF_KV), side(value, core, HALF_KV)), axis=1)
    across = swap(jnp.concatenate(
        (side(query, 1 - core, HALF_Q), side(output_gradient, 1 - core, HALF_Q), side(key, 1 - core, HALF_KV), side(value, 1 - core, HALF_KV)),
        axis=1,
    ))
    u0 = jnp.concatenate((kv_own, across[:, 2 * HALF_Q:]), axis=0)
    u6 = hop(u0, [(s, (s + 6) % CHIPS) for s in range(4)])
    u1 = hop(u0, [(s, s + 1) for s in range(7)])
    u2 = hop(u1, [(s, s + 1) for s in range(1, 7)])

    mine = pl.BlockSpec((T, HALF_Q), lambda i, d, o, p: (0, p[0] & 1))
    stats = struct((CHUNKS, 8, ROWS))
    wide = struct((CHUNKS, D, ROWS))
    stacked = struct((CHUNKS, ROWS, D), jnp.bfloat16)
    unit = struct((UNIT, 2 * HALF_KV), jnp.bfloat16)
    packed = struct((T, 2 * HALF_Q), jnp.bfloat16)
    token_half = struct((T, HALF_Q), jnp.bfloat16)
    held = [pltpu.VMEM(x.shape, x.dtype) for x in (stats, stats, wide)]

    q, do, m0, l0, acc0 = call(
        first_kernel, "own", scalars, (query, output_gradient, across, u0),
        (mine, mine, None, None), (stacked, stacked, stats, stats, wide),
    )
    u5 = hop(after(u6, m0), [((s + 6) % CHIPS, (s + 5) % CHIPS) for s in range(4)])

    def near(units, name, state, held_units, flops=1024):
        return call(
            functools.partial(near_kernel, units), name, scalars, (q, *state, *held_units),
            (None,) * (4 + len(units)), (stats, stats, wide), flops=flops,
        )

    m1, l1, acc1 = near((1,), "near1", (m0, l0, acc0), (u1,))
    u3 = hop(after(u2, m1), [(s, s + 1) for s in range(2, 7)])
    u4 = hop(u5, [(s, (s - 1) % CHIPS) for s in (5, 6, 7, 0)])
    state = near((2, 5), "near25", (m1, l1, acc1), (u2, u5))
    m2, l2, acc2 = near((3,), "near3", state, (u3,), 1 << 31)
    o_own, o_send, lse, delta, dq3, g3, g4 = call(
        middle_kernel, "middle", scalars, (q, do, m2, l2, acc2, u3, u4), (None,) * 7,
        (token_half, token_half, stats, stats, wide, unit, unit), held,
    )

    def back(units, name, dq, held_units):
        n = len(units)
        outs = (unit,) * n + ((token_half, packed) if 0 in units else (wide,))
        return call(
            functools.partial(back_kernel, units), name, scalars, (q, do, lse, delta, dq, *held_units),
            (None,) * (5 + len(held_units)), outs, held[2:] if 0 in units else (),
        )

    def add(*terms):
        total = terms[0].astype(jnp.float32)
        for term in terms[1:]:
            total = total + term.astype(jnp.float32)
        return total.astype(jnp.bfloat16)

    b4 = hop(g4, [(t, (t + 1) % CHIPS) for t in range(4, 8)])
    b3 = hop(g3, [(t, t - 1) for t in range(3, 8)])
    g5, g2, dq2 = back((5, 2), "back52", dq3, (u5, u2))
    a5 = add(g5, b4)
    a2 = add(g2, after(b3, a5))
    r5 = hop(a5, [(t, (t + 3) % CHIPS) for t in (5, 6, 7, 0)])
    b2 = hop(a2, [(t, t - 1) for t in range(2, 8)])
    g1, g0, dq_own, sent = back((1, 0), "back10", after(dq2, a5, a2), (u1, u0, o_send))
    a1 = add(g1, b2)
    r1 = [hop(a1[i * T:(i + 1) * T], [(t, t - 1) for t in range(1, 8)], i) for i in range(2)]
    s05, = call(sum_kernel, "sum05", scalars, (g0, r5), (None, None), (unit,), flops=3 << 31)
    other = swap(after(sent, s05, r1[0], r1[1]))
    def join(own, other):
        return jnp.where(core == 0, jnp.concatenate((own, other), axis=1), jnp.concatenate((other, own), axis=1))

    attn = join(o_own, other[:, :HALF_Q])
    grad_query = join(dq_own, other[:, HALF_Q:])
    s05_other = swap(s05[T:])
    sums = add(s05[:T], after(r1[0], r1[1]))
    sums_other = add(s05_other, r1[1])
    return (
        attn,
        grad_query,
        join(sums[:, :HALF_KV], sums_other[:, :HALF_KV]),
        join(sums[:, HALF_KV:], sums_other[:, HALF_KV:]),
    )


def solution(mesh):
    rows = P(("dp", "ctx"), None)
    return jax.shard_map(
        shards,
        mesh=mesh,
        in_specs=(rows, rows, rows, rows, P("dp"), P("dp")),
        out_specs=(rows, rows, rows, rows),
        check_vma=False,
    )
```
